128 devices in a mesh: dp: 16 (over x_hi, z, core), tensor: 8 (over x_lo, y).
Axes of the slice: x: 4 (x_hi: 2, x_lo: 2; x = x_hi * 2 + x_lo), y: 4, z: 4, core: 2. Of those that a mesh axis runs over, the one named last changes fastest.
Arguments:
- grad_blocks: bfloat16 [256, 512, 512], P(None, ('dp', 'tensor')), may hold values from -1.1953125 to 1.1953125
- block_of_slot: int32 [256], replicated, may hold values from 0 to 255, each once
- left_basis: float32 [256, 512, 512], P(('dp', 'tensor'))
- right_basis: float32 [256, 512, 512], P(('dp', 'tensor'))
- left_gram: float32 [256, 512, 512], P(('dp', 'tensor')), as said below
- right_gram: float32 [256, 512, 512], P(('dp', 'tensor')), as said below
- moment_first: float32 [256, 512, 512], P(('dp', 'tensor')), may hold values from -1.8 to 1.8
- moment_second: float32 [256, 512, 512], P(('dp', 'tensor')), may hold values from 0.01 to 0.2
Outputs:
- update: float32 [256, 512, 512], P(None, ('dp', 'tensor'))
- new_left_gram: float32 [256, 512, 512], P(('dp', 'tensor'))
- new_right_gram: float32 [256, 512, 512], P(('dp', 'tensor'))
- new_first: float32 [256, 512, 512], P(('dp', 'tensor'))
- new_second: float32 [256, 512, 512], P(('dp', 'tensor'))
The draws below stay inside these ranges and needn't reach their ends.
Inputs may be any that keep to these rules, and one draw needn't show every extreme that they name: `block_of_slot`: each block appears in exactly one slot; slot s belongs to the device of flat index s // 2 over dp then tensor. `left_gram`: symmetric. `right_gram`: symmetric.
All inputs are finite; a program needn't handle non-finite values.
Results may differ from the reference program's by a relative error of at most 0.0003.
Values may be sent and summed in bfloat16 or wider, within the bound.
A program may use at most 128 MiB of HBM per device.

```python
import math
import jax
import jax.numpy as jnp
from jax import lax

BS = 512
BLOCKS = 256


def basis_like(key):
    noise = jax.random.normal(key, (BLOCKS, BS, BS), jnp.float32)
    return jnp.eye(BS, dtype=jnp.float32)[None] + 0.8 / math.sqrt(BS) * noise


def gram_like(key):
    first, second = jax.random.split(key)
    noise = jax.random.normal(first, (BLOCKS, BS, BS), jnp.float32) * 0.05
    symmetric = 0.5 * (noise + jnp.swapaxes(noise, 1, 2))
    diag = jax.random.uniform(second, (BLOCKS, 1, BS), jnp.float32, 0.5, 2.0)
    return symmetric + jnp.eye(BS, dtype=jnp.float32)[None] * diag


def draw_left_basis(key, part):
    key = jax.random.fold_in(key, 11)
    return basis_like(key)


def draw_right_basis(key, part):
    key = jax.random.fold_in(key, 23)
    return basis_like(key)


def draw_left_gram(key, part):
    key = jax.random.fold_in(key, 37)
    return gram_like(key)


def draw_right_gram(key, part):
    key = jax.random.fold_in(key, 41)
    return gram_like(key)


def steps_of(own_key, dims, cuts, low, top_value):
    def one(dim, blocks):
        draws = jax.random.uniform(jax.random.fold_in(jax.random.fold_in(own_key, 6), dim), (blocks,), jnp.float32, low / len(cuts), top_value / len(cuts))
        return jnp.repeat(jnp.exp(draws), dims[dim] // blocks).reshape((-1,) + (1,) * (len(dims) - dim - 1))

    loudness = one(*cuts[0])
    for cut in cuts[1:]:
        loudness = loudness * one(*cut)
    return loudness


def centred(stream_key, extent, deviation, most, cuts=(), kind=jnp.bfloat16):
    loudness = steps_of(stream_key, extent, cuts, -0.22, 0.18) if cuts else 1.0
    entries = jax.random.normal(stream_key, extent, jnp.float32) * deviation * loudness
    return jnp.minimum(jnp.maximum(entries, -most), most).astype(kind)


def setup_inputs(seed: int = 0) -> dict:
    key_of = jax.random.split(jax.random.key(seed), 9)
    return {
        "grad_blocks": centred(key_of[0], (BLOCKS, BS, BS), 0.2, 1.1953125, ((1, 128),)),
        "block_of_slot": jax.random.permutation(key_of[1], BLOCKS).astype(jnp.int32),
        "left_basis": draw_left_basis(jax.random.fold_in(key_of[8], 71), 0),
        "right_basis": draw_right_basis(jax.random.fold_in(key_of[8], 71), 0),
        "left_gram": draw_left_gram(jax.random.fold_in(key_of[8], 71), 0),
        "right_gram": draw_right_gram(jax.random.fold_in(key_of[8], 71), 0),
        "moment_first": centred(key_of[6], (BLOCKS, BS, BS), 0.3, 1.8, ((0, 128),), jnp.float32),
        "moment_second": jnp.clip(jnp.exp(math.log(0.2) - 2.9957323 * jax.random.uniform(key_of[7], (BLOCKS, BS, BS), jnp.float32) ** steps_of(key_of[7], (BLOCKS, BS, BS), ((0, 128),), -0.2, 0.2)), 0.01, 0.2),
    }


def soap_block(owned, left, right, lgram, rgram, first, second):
    hi = lax.Precision.HIGHEST
    rotated = jnp.dot(jnp.dot(left.T, owned, precision=hi), right, precision=hi)
    new_first = 0.9 * first + 0.1 * rotated
    new_second = 0.95 * second + 0.05 * rotated * rotated
    normalized = new_first / (jnp.sqrt(new_second) + 1e-08)
    result = jnp.dot(jnp.dot(left, normalized, precision=hi), right.T, precision=hi)
    new_lgram = 0.95 * lgram + 0.05 * jnp.dot(owned, owned.T, precision=hi)
    new_rgram = 0.95 * rgram + 0.05 * jnp.dot(owned.T, owned, precision=hi)
    return (result, new_lgram, new_rgram, new_first, new_second)

def reference(grad_blocks, block_of_slot, left_basis, right_basis, left_gram, right_gram, moment_first, moment_second):

    def one_slot(index):
        owned = lax.dynamic_index_in_dim(grad_blocks, block_of_slot[index].astype(jnp.int32), 0, False).astype(jnp.float32)
        return soap_block(owned, left_basis[index], right_basis[index], left_gram[index], right_gram[index], moment_first[index], moment_second[index])
    result, new_lgram, new_rgram, new_first, new_second = lax.map(one_slot, jnp.arange(BLOCKS, dtype=jnp.int32))
    update = jnp.zeros(result.shape, jnp.float32).at[block_of_slot].set(result)
    return (update, new_lgram, new_rgram, new_first, new_second)
```

```python
import jax
import jax.numpy as jnp
from jax import lax
from jax.experimental import pallas as pl
from jax.experimental.pallas import tpu as pltpu
from jax.sharding import PartitionSpec as P

MESH = pl.DeviceIdType.MESH
F32 = jnp.float32
BF16 = jnp.bfloat16
N = 512
DP, TP = 16, 8
DEV = DP * TP
CH = 128
GROUP = CH // 4
LEVELS = 32767.0


def split(x):
    hi = x.astype(BF16)
    return hi, (x - hi.astype(F32)).astype(BF16)


def dot(a, b):
    return jnp.dot(a, b, preferred_element_type=F32)


def dot_nt(a, b):
    return lax.dot_general(a, b, (((1,), (1,)), ((), ())), preferred_element_type=F32)


def dot_tn(a, b):
    return lax.dot_general(a, b, (((0,), (0,)), ((), ())), preferred_element_type=F32)


def exchange_kernel(
    bos,
    grad,
    left_h,
    right_h,
    lgram_h,
    rgram_h,
    first_h,
    second_h,
    codes,
    scales,
    nlgram,
    nrgram,
    nfirst,
    nsecond,
    left,
    right,
    lgram,
    rgram,
    first,
    second,
    lt_hi,
    lt_lo,
    l_hi,
    l_lo,
    r_hi,
    r_lo,
    stage_in,
    land_in,
    owned,
    n_hi,
    n_lo,
    stage_out,
    stage_scale,
    load_sem,
    in_send,
    in_recv,
    out_send,
    out_recv,
    sc_sem,
):
    dp = lax.axis_index("dp")
    tp = lax.axis_index("tensor")
    me = dp * TP + tp

    loads = [
        pltpu.make_async_copy(src, dst, load_sem.at[i])
        for i, (src, dst) in enumerate(
            ((left_h, left), (right_h, right), (first_h, first), (second_h, second), (lgram_h, lgram), (rgram_h, rgram))
        )
    ]
    for load in loads:
        load.start()

    barrier = pltpu.get_barrier_semaphore()

    def greet(d, t):
        pl.semaphore_signal(barrier, inc=1, device_id=(d, t), device_id_type=MESH)

    for i in range(1, TP):
        greet(dp, (tp + i) & (TP - 1))

    @pl.loop(1, DP)
    def _(j):
        for i in range(TP):
            greet((dp + j) & (DP - 1), (tp + i) & (TP - 1))

    for s in range(2):

        @pl.loop(0, DEV, step=8)
        def _(p):
            for i in range(8):
                stage_in[s, p + i] = grad[bos[2 * (p + i) + s]]

        land_in[s, me] = stage_in[s, me]

    pl.semaphore_wait(barrier, DEV - 1)

    def send_in(s, d, t):
        pltpu.make_async_remote_copy(
            stage_in.at[s, d * TP + t],
            land_in.at[s, me],
            in_send.at[s],
            in_recv.at[s],
            device_id=(d, t),
            device_id_type=MESH,
        ).start()

    for s in range(2):
        for i in range(1, TP):
            send_in(s, dp, (tp + i) & (TP - 1))

        @pl.loop(1, DP)
        def _(j):
            for i in range(TP):
                send_in(s, (dp + j) & (DP - 1), (tp + i) & (TP - 1))

    loads[0].wait()
    loads[1].wait()
    for s in range(2):

        @pl.loop(0, N, step=CH)
        def _(r):
            rows = pl.ds(pl.multiple_of(r, CH), CH)
            hi, lo = split(left[s, rows, :])
            l_hi[s, rows, :] = hi
            l_lo[s, rows, :] = lo
            hi, lo = split(right[s, rows, :])
            r_hi[s, rows, :] = hi
            r_lo[s, rows, :] = lo
            hi, lo = split(left[s, :, rows].T)
            lt_hi[s, rows, :] = hi
            lt_lo[s, rows, :] = lo

    loads[2].wait()
    loads[3].wait()

    def all_of(ref, sem):
        pltpu.make_async_copy(ref, ref, sem).wait()

    for s in range(2):
        all_of(land_in.at[s, pl.ds(0, DEV - 1)], in_recv.at[s])
        for c in range(4):
            owned[s, :, c * 128 : (c + 1) * 128] = land_in[s, :, 4 * c : 4 * c + 4, :].reshape(N, 128)

        @pl.loop(0, N, step=CH)
        def _(r):
            rows = pl.ds(pl.multiple_of(r, CH), CH)
            block = owned[s]
            a = dot(lt_hi[s, rows, :], block) + dot(lt_lo[s, rows, :], block)
            a_hi, a_lo = split(a)
            rotated = dot(a_hi, r_hi[s]) + (dot(a_hi, r_lo[s]) + dot(a_lo, r_hi[s]))
            nf = 0.9 * first[s, rows, :] + 0.1 * rotated
            ns = 0.95 * second[s, rows, :] + 0.05 * rotated * rotated
            nfirst[s, rows, :] = nf
            nsecond[s, rows, :] = ns
            hi, lo = split(nf / (jnp.sqrt(ns) + 1e-08))
            n_hi[rows, :] = hi
            n_lo[rows, :] = lo

        @pl.loop(0, N // CH)
        def _(j):
            chunk = (dp // (GROUP // TP) + j) & (N // CH - 1)
            rows = pl.ds(pl.multiple_of(chunk * CH, CH), CH)
            b = dot(l_hi[s, rows, :], n_hi[...]) + (dot(l_hi[s, rows, :], n_lo[...]) + dot(l_lo[s, rows, :], n_hi[...]))
            b_hi, b_lo = split(b)
            result = dot_nt(b_hi, r_hi[s]) + (dot_nt(b_hi, r_lo[s]) + dot_nt(b_lo, r_hi[s]))
            top = jnp.maximum(jnp.max(jnp.abs(result), axis=1, keepdims=True), 1e-33)
            q = jnp.clip(jnp.round(result * (LEVELS / top)), -LEVELS, LEVELS).astype(jnp.int32)
            packed = (q[:, : N // 2] & 0xFFFF) | (q[:, N // 2 :] << 16)
            first_dev = pl.multiple_of(chunk * GROUP, GROUP)
            for c in range(2):
                stage_out[s, pl.ds(first_dev, GROUP), 4 * c : 4 * c + 4, :] = packed[
                    :, c * 128 : (c + 1) * 128
                ].reshape(GROUP, 4, 128)
            step = jnp.broadcast_to(top * (1.0 / LEVELS), (CH, 128)).T
            stage_scale[chunk, s] = step[:1, :]

            @pl.loop(0, GROUP // TP)
            def _(g):
                d = chunk * (GROUP // TP) + ((dp + g) & (GROUP // TP - 1))
                for i in range(TP):
                    t = (tp + i) & (TP - 1)

                    def send_out():
                        pltpu.make_async_remote_copy(
                            stage_out.at[s, d * TP + t],
                            codes.at[s, me],
                            out_send.at[s],
                            out_recv.at[s],
                            device_id=(d, t),
                            device_id_type=MESH,
                        ).start()
                        if s == 1:
                            pltpu.make_async_remote_copy(
                                stage_scale.at[chunk],
                                scales.at[me],
                                sc_sem.at[0],
                                sc_sem.at[1],
                                device_id=(d, t),
                                device_id_type=MESH,
                            ).start()

                    if i:
                        send_out()
                    else:
                        pl.when(d != dp)(send_out)

        codes[s, me] = stage_out[s, me]

    scales[me] = stage_scale[dp // (GROUP // TP)]

    loads[4].wait()
    loads[5].wait()
    for s in range(2):

        @pl.loop(0, N, step=CH)
        def _(r):
            rows = pl.ds(pl.multiple_of(r, CH), CH)
            nlgram[s, rows, :] = 0.95 * lgram[s, rows, :] + 0.05 * dot_nt(owned[s, rows, :], owned[s])
            nrgram[s, rows, :] = 0.95 * rgram[s, rows, :] + 0.05 * dot_tn(owned[s, :, rows], owned[s])

    for s in range(2):
        all_of(land_in.at[s, pl.ds(0, DEV - 1)], in_send.at[s])
        all_of(codes.at[s, pl.ds(0, DEV - 1)], out_send.at[s])
        all_of(codes.at[s, pl.ds(0, DEV - 1)], out_recv.at[s])
        all_of(scales.at[pl.ds(0, DEV - 1)], sc_sem.at[s])


def finish_kernel(bos, codes, scales, nlgram, nrgram, nfirst, nsecond, update, o_l, o_r, o_f, o_s, upd, sem):
    me = lax.axis_index("dp") * TP + lax.axis_index("tensor")
    moves = [
        pltpu.make_async_copy(src, dst, sem.at[i])
        for i, (src, dst) in enumerate(((nlgram, o_l), (nrgram, o_r), (nfirst, o_f), (nsecond, o_s)))
    ]
    for move in moves:
        move.start()
    lane = lax.broadcasted_iota(jnp.int32, (8, 128), 1)
    row = lax.broadcasted_iota(jnp.int32, (8, 128), 0)
    mine = lane == (me & (GROUP - 1)) * 4 + (row & 3)

    for s in range(2):

        @pl.loop(0, DEV, step=8)
        def _(p):
            for i in range(8):
                b = bos[2 * (p + i) + s]
                v = codes[s, p + i]
                step = jnp.sum(
                    jnp.where(mine, jnp.broadcast_to(scales[p + i, s], (8, 128)), 0.0), axis=1, keepdims=True
                )
                upd[b, 0:8, :] = ((v << 16) >> 16).astype(F32) * step
                upd[b, 8:16, :] = (v >> 16).astype(F32) * step

    out = pltpu.make_async_copy(upd, update, sem.at[4])
    out.start()
    for move in moves:
        move.wait()
    out.wait()


def local(grad_blocks, block_of_slot, left_basis, right_basis, left_gram, right_gram, moment_first, moment_second):
    blocks = grad_blocks.shape[0]
    grad = grad_blocks.reshape(blocks, 4, 4, 128).transpose(0, 2, 1, 3).reshape(blocks, 16, 128)
    hbm = pl.BlockSpec(memory_space=pltpu.HBM)
    vmem = pl.BlockSpec(memory_space=pltpu.VMEM)
    smem = pl.BlockSpec(memory_space=pltpu.SMEM)
    square = (2, N, N)
    codes, scales, nlgram, nrgram, nfirst, nsecond = pl.pallas_call(
        exchange_kernel,
        out_shape=(
            pltpu.VMEM((2, DEV, 8, 128), jnp.int32),
            pltpu.VMEM((DEV, 2, 1, 128), F32),
            pltpu.VMEM(square, F32),
            pltpu.VMEM(square, F32),
            pltpu.VMEM(square, F32),
            pltpu.VMEM(square, F32),
        ),
        in_specs=[smem, vmem] + [hbm] * 6,
        out_specs=(vmem,) * 6,
        scratch_shapes=[pltpu.VMEM(square, F32)] * 6
        + [pltpu.VMEM(square, BF16)] * 6
        + [
            pltpu.VMEM((2, DEV, 16, 128), BF16),
            pltpu.VMEM((2, DEV, 16, 128), BF16),
            pltpu.VMEM(square, BF16),
            pltpu.VMEM((N, N), BF16),
            pltpu.VMEM((N, N), BF16),
            pltpu.VMEM((2, DEV, 8, 128), jnp.int32),
            pltpu.VMEM((N // CH, 2, 1, 128), F32),
            pltpu.SemaphoreType.DMA((6,)),
            pltpu.SemaphoreType.DMA((2,)),
            pltpu.SemaphoreType.DMA((2,)),
            pltpu.SemaphoreType.DMA((2,)),
            pltpu.SemaphoreType.DMA((2,)),
            pltpu.SemaphoreType.DMA((2,)),
        ],
        compiler_params=pltpu.CompilerParams(collective_id=0, has_side_effects=True, vmem_limit_bytes=40 << 20),
        name="exchange",
    )(block_of_slot, grad, left_basis, right_basis, left_gram, right_gram, moment_first, moment_second)
    update, *rest = pl.pallas_call(
        finish_kernel,
        out_shape=(jax.ShapeDtypeStruct((blocks, 16, 128), F32),) + (jax.ShapeDtypeStruct(square, F32),) * 4,
        in_specs=[smem] + [vmem] * 6,
        out_specs=(hbm,) * 5,
        scratch_shapes=[pltpu.VMEM((blocks, 16, 128), F32), pltpu.SemaphoreType.DMA((5,))],
        compiler_params=pltpu.CompilerParams(vmem_limit_bytes=16 << 20),
        name="finish",
    )(block_of_slot, codes, scales, nlgram, nrgram, nfirst, nsecond)
    update = update.reshape(blocks, 4, 4, 128).transpose(0, 2, 1, 3).reshape(blocks, 4, N)
    return (update, *rest)


def solution(mesh):
    owner = P(("dp", "tensor"), None, None)
    rows = P(None, ("dp", "tensor"), None)
    return jax.shard_map(
        local,
        mesh=mesh,
        in_specs=(rows, P(), owner, owner, owner, owner, owner, owner),
        out_specs=(rows, owner, owner, owner, owner),
        check_vma=False,
    )
```

```python
import jax
import jax.numpy as jnp
from jax import lax
from jax.experimental import pallas as pl
from jax.experimental.pallas import tpu as pltpu
from jax.sharding import PartitionSpec as P

MESH = pl.DeviceIdType.MESH
F32 = jnp.float32
BF16 = jnp.bfloat16
N = 512
DP, TP = 16, 8
DEV = DP * TP
LEVELS = 32767.0


def split(x):
    hi = x.astype(BF16)
    return hi, (x - hi.astype(F32)).astype(BF16)


def dot(a, b):
    return jnp.dot(a, b, preferred_element_type=F32)


def dot_nt(a, b):
    return lax.dot_general(a, b, (((1,), (1,)), ((), ())), preferred_element_type=F32)


def dot_tn(a, b):
    return lax.dot_general(a, b, (((0,), (0,)), ((), ())), preferred_element_type=F32)


def exchange_kernel(
    bos_h,
    grad_h,
    left_h,
    right_h,
    lgram_h,
    rgram_h,
    first_h,
    second_h,
    codes,
    scales,
    nlgram,
    nrgram,
    nfirst,
    nsecond,
    bos,
    grad,
    left,
    right,
    lgram,
    rgram,
    first,
    second,
    lt_hi,
    lt_lo,
    l_hi,
    l_lo,
    r_hi,
    r_lo,
    stage_in,
    land_in,
    owned,
    b_hi,
    b_lo,
    stage_out,
    stage_scale,
    load_sem,
    in_send,
    in_recv,
    out_send,
    out_recv,
    sc_sem,
):
    dp = lax.axis_index("dp")
    tp = lax.axis_index("tensor")
    me = dp * TP + tp

    loads = [
        pltpu.make_async_copy(src, dst, load_sem.at[i])
        for i, (src, dst) in enumerate(
            (
                (bos_h, bos),
                (grad_h, grad),
                (left_h, left),
                (right_h, right),
                (first_h, first),
                (second_h, second),
                (lgram_h, lgram),
                (rgram_h, rgram),
            )
        )
    ]
    for load in loads:
        load.start()

    barrier = pltpu.get_barrier_semaphore()

    def greet(d, t):
        pl.semaphore_signal(barrier, inc=1, device_id=(d, t), device_id_type=MESH)

    for i in range(1, TP):
        greet(dp, (tp + i) & (TP - 1))

    @pl.loop(1, DP)
    def _(j):
        for i in range(TP):
            greet((dp + j) & (DP - 1), (tp + i) & (TP - 1))

    loads[0].wait()
    loads[1].wait()
    for s in range(2):

        @pl.loop(0, DEV, step=8)
        def _(p):
            for i in range(8):
                stage_in[s, p + i] = grad[bos[2 * (p + i) + s]]

        land_in[s, me] = stage_in[s, me]

    pl.semaphore_wait(barrier, DEV - 1)

    def send_in(s, d, t):
        pltpu.make_async_remote_copy(
            stage_in.at[s, d * TP + t],
            land_in.at[s, me],
            in_send.at[s],
            in_recv.at[s],
            device_id=(d, t),
            device_id_type=MESH,
        ).start()

    for s in range(2):
        for i in range(1, TP):
            send_in(s, dp, (tp + i) & (TP - 1))

        @pl.loop(1, DP)
        def _(j):
            for i in range(TP):
                send_in(s, (dp + j) & (DP - 1), (tp + i) & (TP - 1))

    loads[2].wait()
    loads[3].wait()
    for s in range(2):

        @pl.loop(0, N, step=128)
        def _(r):
            rows = pl.ds(pl.multiple_of(r, 128), 128)
            hi, lo = split(left[s, rows, :])
            l_hi[s, rows, :] = hi
            l_lo[s, rows, :] = lo
            hi, lo = split(right[s, rows, :])
            r_hi[s, rows, :] = hi
            r_lo[s, rows, :] = lo
            hi, lo = split(left[s, :, rows].T)
            lt_hi[s, rows, :] = hi
            lt_lo[s, rows, :] = lo

    loads[4].wait()
    loads[5].wait()

    def all_of(ref, sem):
        pltpu.make_async_copy(ref, ref, sem).wait()

    for s in range(2):
        all_of(land_in.at[s, pl.ds(0, DEV - 1)], in_recv.at[s])
        for c in range(4):
            owned[s, :, c * 128 : (c + 1) * 128] = land_in[s, :, 4 * c : 4 * c + 4, :].reshape(N, 128)

        block = owned[s]
        a_hi, a_lo = split(dot(lt_hi[s], block) + dot(lt_lo[s], block))
        rotated = dot(a_hi, r_hi[s]) + (dot(a_hi, r_lo[s]) + dot(a_lo, r_hi[s]))
        nf = 0.9 * first[s] + 0.1 * rotated
        ns = 0.95 * second[s] + 0.05 * rotated * rotated
        nfirst[s] = nf
        nsecond[s] = ns
        n_hi, n_lo = split(nf / (jnp.sqrt(ns) + 1e-08))
        hi, lo = split(dot(l_hi[s], n_hi) + (dot(l_hi[s], n_lo) + dot(l_lo[s], n_hi)))
        b_hi[...] = hi.reshape(b_hi.shape)
        b_lo[...] = lo.reshape(b_lo.shape)

        for j in range(2):
            c = (dp + j) & 1
            hi = b_hi[:, c].reshape(N // 2, N)
            lo = b_lo[:, c].reshape(N // 2, N)
            result = dot_nt(hi, r_hi[s]) + (dot_nt(hi, r_lo[s]) + dot_nt(lo, r_hi[s]))
            top = jnp.maximum(jnp.max(jnp.abs(result), axis=1, keepdims=True), 1e-33)
            q = jnp.clip(jnp.round(result * (LEVELS / top)), -LEVELS, LEVELS).astype(jnp.int32)
            packed = (q[:, : N // 2] & 0xFFFF) | (q[:, N // 2 :] << 16)
            for h in range(2):
                stage_out[s, :, c, :, 4 * h : 4 * h + 4, :] = packed[:, h * 128 : (h + 1) * 128].reshape(
                    DP // 2, TP, 4, 128
                )
            step = jnp.broadcast_to(top * (1.0 / LEVELS), (N // 2, 128)).T
            for h in range(2):
                stage_scale[c, h, s] = step[:1, h * 128 : (h + 1) * 128]

            def send_out(g, t):
                pltpu.make_async_remote_copy(
                    stage_out.at[s, g, c, t],
                    codes.at[s, me],
                    out_send.at[s],
                    out_recv.at[s],
                    device_id=(2 * g + c, t),
                    device_id_type=MESH,
                ).start()
                if s == 1:
                    pltpu.make_async_remote_copy(
                        stage_scale.at[c, g // 4],
                        scales.at[me],
                        sc_sem.at[0],
                        sc_sem.at[1],
                        device_id=(2 * g + c, t),
                        device_id_type=MESH,
                    ).start()

            for i in range(1 if j == 0 else 0, TP):
                send_out(dp // 2, (tp + i) & (TP - 1))

            @pl.loop(1, DP // 2)
            def _(a):
                for i in range(TP):
                    send_out((dp // 2 + a) & (DP // 2 - 1), (tp + i) & (TP - 1))

        codes[s, me] = stage_out[s, dp // 2, dp & 1, tp]

    scales[me] = stage_scale[dp & 1, dp // 8]

    loads[6].wait()
    loads[7].wait()
    for s in range(2):
        nlgram[s] = 0.95 * lgram[s] + 0.05 * dot_nt(owned[s], owned[s])
        nrgram[s] = 0.95 * rgram[s] + 0.05 * dot_tn(owned[s], owned[s])

    for s in range(2):
        all_of(land_in.at[s, pl.ds(0, DEV - 1)], in_send.at[s])
        all_of(codes.at[s, pl.ds(0, DEV - 1)], out_send.at[s])
        all_of(codes.at[s, pl.ds(0, DEV - 1)], out_recv.at[s])
        all_of(scales.at[pl.ds(0, DEV - 1)], sc_sem.at[s])


def finish_kernel(bos_h, codes, scales, nlgram, nrgram, nfirst, nsecond, update, o_l, o_r, o_f, o_s, bos, upd, sem):
    dp = lax.axis_index("dp")
    tp = lax.axis_index("tensor")
    load = pltpu.make_async_copy(bos_h, bos, sem.at[5])
    load.start()
    moves = [
        pltpu.make_async_copy(src, dst, sem.at[i])
        for i, (src, dst) in enumerate(((nlgram, o_l), (nrgram, o_r), (nfirst, o_f), (nsecond, o_s)))
    ]
    for move in moves:
        move.start()
    lane = lax.broadcasted_iota(jnp.int32, (8, 128), 1)
    row = lax.broadcasted_iota(jnp.int32, (8, 128), 0)
    mine = lane == (((dp // 2) & 3) * TP + tp) * 4 + (row & 3)
    load.wait()

    for s in range(2):

        @pl.loop(0, DEV, step=32)
        def _(p):
            for i in range(32):
                b = bos[2 * (p + i) + s]
                v = codes[s, p + i]
                step = jnp.sum(
                    jnp.where(mine, jnp.broadcast_to(scales[p + i, s], (8, 128)), 0.0), axis=1, keepdims=True
                )
                upd[b, 0:8, :] = ((v << 16) >> 16).astype(F32) * step
                upd[b, 8:16, :] = (v >> 16).astype(F32) * step

    out = pltpu.make_async_copy(upd, update, sem.at[4])
    out.start()
    for move in moves:
        move.wait()
    out.wait()


def local(grad_blocks, block_of_slot, left_basis, right_basis, left_gram, right_gram, moment_first, moment_second):
    blocks = grad_blocks.shape[0]
    grad = grad_blocks.reshape(blocks, 4, 4, 128).transpose(0, 2, 1, 3).reshape(blocks, 16, 128)
    hbm = pl.BlockSpec(memory_space=pltpu.HBM)
    vmem = pl.BlockSpec(memory_space=pltpu.VMEM)
    square = (2, N, N)
    operands = [
        pltpu.with_memory_space_constraint(x, pltpu.HBM)
        for x in (
            block_of_slot,
            grad,
            left_basis,
            right_basis,
            left_gram,
            right_gram,
            moment_first,
            moment_second,
        )
    ]
    codes, scales, nlgram, nrgram, nfirst, nsecond = pl.pallas_call(
        exchange_kernel,
        out_shape=(
            pltpu.VMEM((2, DEV, 8, 128), jnp.int32),
            pltpu.VMEM((DEV, 2, 1, 128), F32),
            pltpu.VMEM(square, F32),
            pltpu.VMEM(square, F32),
            pltpu.VMEM(square, F32),
            pltpu.VMEM(square, F32),
        ),
        in_specs=[hbm] * 8,
        out_specs=(vmem,) * 6,
        scratch_shapes=[pltpu.SMEM((blocks,), jnp.int32), pltpu.VMEM((blocks, 16, 128), BF16)]
        + [pltpu.VMEM(square, F32)] * 6
        + [pltpu.VMEM(square, BF16)] * 6
        + [
            pltpu.VMEM((2, DEV, 16, 128), BF16),
            pltpu.VMEM((2, DEV, 16, 128), BF16),
            pltpu.VMEM(square, BF16),
            pltpu.VMEM((DP // 2, 2, 4 * TP, N), BF16),
            pltpu.VMEM((DP // 2, 2, 4 * TP, N), BF16),
            pltpu.VMEM((2, DP // 2, 2, TP, 8, 128), jnp.int32),
            pltpu.VMEM((2, 2, 2, 1, 128), F32),
            pltpu.SemaphoreType.DMA((8,)),
            pltpu.SemaphoreType.DMA((2,)),
            pltpu.SemaphoreType.DMA((2,)),
            pltpu.SemaphoreType.DMA((2,)),
            pltpu.SemaphoreType.DMA((2,)),
            pltpu.SemaphoreType.DMA((2,)),
        ],
        compiler_params=pltpu.CompilerParams(collective_id=0, has_side_effects=True, vmem_limit_bytes=44 << 20),
        name="exchange",
    )(*operands)
    update, *rest = pl.pallas_call(
        finish_kernel,
        out_shape=(jax.ShapeDtypeStruct((blocks, 16, 128), F32),) + (jax.ShapeDtypeStruct(square, F32),) * 4,
        in_specs=[hbm] + [vmem] * 6,
        out_specs=(hbm,) * 5,
        scratch_shapes=[
            pltpu.SMEM((blocks,), jnp.int32),
            pltpu.VMEM((blocks, 16, 128), F32),
            pltpu.SemaphoreType.DMA((6,)),
        ],
        compiler_params=pltpu.CompilerParams(vmem_limit_bytes=16 << 20),
        name="finish",
    )(operands[0], codes, scales, nlgram, nrgram, nfirst, nsecond)
    update = update.reshape(blocks, 4, 4, 128).transpose(0, 2, 1, 3).reshape(blocks, 4, N)
    return (update, *rest)


def solution(mesh):
    owner = P(("dp", "tensor"), None, None)
    rows = P(None, ("dp", "tensor"), None)
    return jax.shard_map(
        local,
        mesh=mesh,
        in_specs=(rows, P(), owner, owner, owner, owner, owner, owner),
        out_specs=(rows, owner, owner, owner, owner),
        check_vma=False,
    )
```

```python
import jax
import jax.numpy as jnp
from jax import lax
from jax.experimental import pallas as pl
from jax.experimental.pallas import tpu as pltpu
from jax.sharding import PartitionSpec as P

MESH = pl.DeviceIdType.MESH
F32 = jnp.float32
BF16 = jnp.bfloat16
N = 512
DP, TP = 16, 8
DEV = DP * TP
LEVELS = 32767.0


def split(x):
    hi = x.astype(BF16)
    return hi, (x - hi.astype(F32)).astype(BF16)


def dot(a, b):
    return jnp.dot(a, b, preferred_element_type=F32)


def dot_nt(a, b):
    return lax.dot_general(a, b, (((1,), (1,)), ((), ())), preferred_element_type=F32)


def dot_tn(a, b):
    return lax.dot_general(a, b, (((0,), (0,)), ((), ())), preferred_element_type=F32)


def scale_lanes(dp, tp, s):
    lane = lax.broadcasted_iota(jnp.int32, (8, 128), 1)
    row = lax.broadcasted_iota(jnp.int32, (8, 128), 0)
    return lane == 64 * s + (((dp // 2) & 1) * TP + tp) * 4 + (row & 3)


def decode(code, scale, mine):
    step = jnp.sum(jnp.where(mine, jnp.broadcast_to(scale, (8, 128)), 0.0), axis=1, keepdims=True)
    return ((code << 16) >> 16).astype(F32) * step, (code >> 16).astype(F32) * step


def exchange_kernel(
    bos_h,
    grad_h,
    left_h,
    right_h,
    lgram_h,
    rgram_h,
    first_h,
    second_h,
    codes,
    scales,
    rows_of_first,
    nlgram,
    nrgram,
    nfirst,
    nsecond,
    bos,
    grad,
    left,
    right,
    lgram,
    rgram,
    first,
    second,
    lt_hi,
    lt_lo,
    l_hi,
    l_lo,
    r_hi,
    r_lo,
    stage_in,
    land_in,
    owned,
    n_hi,
    n_lo,
    stage_out,
    stage_scale,
    step_of_first,
    load_sem,
    in_send,
    in_recv,
    out_send,
    out_recv,
    sc_sem,
):
    dp = lax.axis_index("dp")
    tp = lax.axis_index("tensor")
    me = dp * TP + tp

    loads = [
        pltpu.make_async_copy(src, dst, load_sem.at[i])
        for i, (src, dst) in enumerate(
            (
                (bos_h, bos),
                (grad_h, grad),
                (left_h, left),
                (right_h, right),
                (first_h, first),
                (second_h, second),
                (lgram_h, lgram),
                (rgram_h, rgram),
            )
        )
    ]
    for load in loads[:2]:
        load.start()

    barrier = pltpu.get_barrier_semaphore()

    def greet(d, t):
        pl.semaphore_signal(barrier, inc=1, device_id=(d, t), device_id_type=MESH)

    for i in range(1, TP):
        greet(dp, (tp + i) & (TP - 1))

    @pl.loop(1, DP)
    def _(j):
        for i in range(TP):
            greet((dp + j) & (DP - 1), (tp + i) & (TP - 1))

    for load in loads[2:]:
        load.start()

    loads[0].wait()
    loads[1].wait()
    for s in range(2):

        @pl.loop(0, DEV, step=8)
        def _(p):
            for i in range(8):
                stage_in[s, p + i] = grad[bos[2 * (p + i) + s]]

        land_in[s, dp // 2, dp & 1, tp] = stage_in[s, me]

    pl.semaphore_wait(barrier, DEV - 1)

    parts = ((2, 4, 6, 0), (8, 10, 12, 14), (1, 3, 5, 7), (9, 11, 13, 15))

    def send_in(s, part):
        def one(d, t):
            pltpu.make_async_remote_copy(
                stage_in.at[s, d * TP + t],
                land_in.at[s, dp // 2, dp & 1, tp],
                in_send.at[s, part],
                in_recv.at[s, part // 2],
                device_id=(d, t),
                device_id_type=MESH,
            ).start()

        for j in parts[part]:
            for i in range(TP):
                if i or j:
                    one((dp + j) & (DP - 1), (tp + i) & (TP - 1))

    def all_of(ref, sem):
        pltpu.make_async_copy(ref, ref, sem).wait()

    def sent_in(s, part):
        count = TP * len(parts[part]) - (0 in parts[part])
        all_of(stage_in.at[s, pl.ds(0, count)], in_send.at[s, part])

    for part in range(4):
        send_in(0, part)

    loads[2].wait()
    loads[3].wait()
    for s in range(2):

        @pl.loop(0, 4)
        def _(r):
            rows = pl.ds(pl.multiple_of(r * 128, 128), 128)
            hi, lo = split(right[s, rows, :])
            r_hi[s, rows, :] = hi
            r_lo[s, rows, :] = lo
            hi, lo = split(left[s, pl.ds(2 * r, 2)])
            l_hi[s, pl.ds(2 * r, 2)] = hi
            l_lo[s, pl.ds(2 * r, 2)] = lo
            for c in range(2):
                hi, lo = split(left[s, :, c, :, rows].reshape(N // 2, 128).T)
                lt_hi[s, c, rows, :] = hi
                lt_lo[s, c, rows, :] = lo

    loads[4].wait()
    loads[5].wait()

    for part in range(3):
        sent_in(0, part)
    send_in(1, 0)
    sent_in(0, 3)
    for part in range(1, 4):
        send_in(1, part)

    for s in range(2):
        half = []
        for j in range(2):
            c = (dp + j) & 1
            all_of(stage_in.at[s, pl.ds(0, DEV // 2 - 1 + j)], in_recv.at[s, j])
            for k in range(4):
                owned[s, :, c, :, k * 128 : (k + 1) * 128] = land_in[s, :, c, :, 4 * k : 4 * k + 4, :].reshape(
                    DP // 2, 4 * TP, 128
                )
            block = owned[s, :, c].reshape(N // 2, N)
            half.append(dot(lt_hi[s, c], block) + dot(lt_lo[s, c], block))
        a_hi, a_lo = split(half[0] + half[1])
        rotated = dot(a_hi, r_hi[s]) + (dot(a_hi, r_lo[s]) + dot(a_lo, r_hi[s]))
        nf = 0.9 * first[s] + 0.1 * rotated
        ns = 0.95 * second[s] + 0.05 * rotated * rotated
        nfirst[s] = nf
        nsecond[s] = ns
        hi, lo = split(nf / (jnp.sqrt(ns) + 1e-08))
        n_hi[...] = hi
        n_lo[...] = lo

        for j in range(2):
            c = (dp + j) & 1
            left_hi = l_hi[s, :, c].reshape(N // 2, N)
            left_lo = l_lo[s, :, c].reshape(N // 2, N)
            hi, lo = split(dot(left_hi, n_hi[...]) + (dot(left_hi, n_lo[...]) + dot(left_lo, n_hi[...])))
            result = dot_nt(hi, r_hi[s]) + (dot_nt(hi, r_lo[s]) + dot_nt(lo, r_hi[s]))
            top = jnp.maximum(jnp.max(jnp.abs(result), axis=1, keepdims=True), 1e-33)
            q = jnp.clip(jnp.round(result * (LEVELS / top)), -LEVELS, LEVELS).astype(jnp.int32)
            packed = (q[:, : N // 2] & 0xFFFF) | (q[:, N // 2 :] << 16)
            for h in range(2):
                stage_out[s, :, c, :, 4 * h : 4 * h + 4, :] = packed[:, h * 128 : (h + 1) * 128].reshape(
                    DP // 2, TP, 4, 128
                )
            step = jnp.broadcast_to(top * (1.0 / LEVELS), (N // 2, 128)).T
            if s == 0:
                step_of_first[c] = step[:1, :]
            else:
                for h in range(4):
                    part = slice(64 * h, 64 * h + 64)
                    stage_scale[c, h] = jnp.concatenate([step_of_first[c][:, part], step[:1, part]], axis=1)

            def send_out(g, t):
                pltpu.make_async_remote_copy(
                    stage_out.at[s, g, c, t],
                    codes.at[s, me],
                    out_send.at[s],
                    out_recv.at[s],
                    device_id=(2 * g + c, t),
                    device_id_type=MESH,
                ).start()

            def send_scale(g, t):
                pltpu.make_async_remote_copy(
                    stage_scale.at[c, g // 2],
                    scales.at[me],
                    sc_sem.at[0],
                    sc_sem.at[1],
                    device_id=(2 * g + c, t),
                    device_id_type=MESH,
                ).start()

            def to_all(send):
                for i in range(1 if j == 0 else 0, TP):
                    send(dp // 2, (tp + i) & (TP - 1))

                @pl.loop(1, DP // 2)
                def _(a):
                    for i in range(TP):
                        send((dp // 2 + a) & (DP // 2 - 1), (tp + i) & (TP - 1))

            if s == 1:
                to_all(send_scale)
            to_all(send_out)

        codes[s, me] = stage_out[s, dp // 2, dp & 1, tp]

    scales[me] = stage_scale[dp & 1, dp // 4]

    loads[6].wait()
    loads[7].wait()
    for s in range(2):
        block = owned[s].reshape(N, N)
        nlgram[s] = 0.95 * lgram[s] + 0.05 * dot_nt(block, block)
        nrgram[s] = 0.95 * rgram[s] + 0.05 * dot_tn(block, block)
    all_of(scales.at[pl.ds(0, DEV - 1)], sc_sem.at[1])
    all_of(codes.at[0, pl.ds(0, DEV - 1)], out_recv.at[0])
    mine = scale_lanes(dp, tp, 0)

    @pl.loop(0, DEV, step=32)
    def _(p):
        for i in range(32):
            low, high = decode(codes[0, p + i], scales[p + i], mine)
            rows_of_first[p + i, 0:8, :] = low
            rows_of_first[p + i, 8:16, :] = high

    for part in range(4):
        sent_in(1, part)
    all_of(scales.at[pl.ds(0, DEV - 1)], sc_sem.at[0])
    for s in range(2):
        all_of(codes.at[s, pl.ds(0, DEV - 1)], out_send.at[s])
    all_of(codes.at[1, pl.ds(0, DEV - 1)], out_recv.at[1])


def finish_kernel(
    bos_h, codes, scales, rows_of_first, nlgram, nrgram, nfirst, nsecond, update, o_l, o_r, o_f, o_s, bos, rows, sem
):
    dp = lax.axis_index("dp")
    tp = lax.axis_index("tensor")
    load = pltpu.make_async_copy(bos_h, bos, sem.at[5])
    load.start()
    moves = [
        pltpu.make_async_copy(src, dst, sem.at[i])
        for i, (src, dst) in enumerate(((nlgram, o_l), (nrgram, o_r), (nfirst, o_f), (nsecond, o_s)))
    ]
    for move in moves:
        move.start()
    mine = scale_lanes(dp, tp, 1)
    load.wait()

    @pl.loop(0, DEV, step=32)
    def _(p):
        for i in range(32):
            pltpu.make_async_copy(rows_of_first.at[p + i], update.at[bos[2 * (p + i)]], sem.at[4]).start()

    @pl.loop(0, DEV, step=32)
    def _(p):
        for i in range(32):
            low, high = decode(codes[1, p + i], scales[p + i], mine)
            rows[p + i, 0:8, :] = low
            rows[p + i, 8:16, :] = high
        for i in range(32):
            pltpu.make_async_copy(rows.at[p + i], update.at[bos[2 * (p + i) + 1]], sem.at[4]).start()

    for move in moves:
        move.wait()
    pltpu.make_async_copy(update, update, sem.at[4]).wait()


def local(grad_blocks, block_of_slot, left_basis, right_basis, left_gram, right_gram, moment_first, moment_second):
    blocks = grad_blocks.shape[0]
    grad = grad_blocks.reshape(blocks, 4, 4, 128).transpose(0, 2, 1, 3).reshape(blocks, 16, 128)
    hbm = pl.BlockSpec(memory_space=pltpu.HBM)
    vmem = pl.BlockSpec(memory_space=pltpu.VMEM)
    square = (2, N, N)
    by_core = (2, DP // 2, 2, 4 * TP, N)
    operands = [
        pltpu.with_memory_space_constraint(x, pltpu.HBM)
        for x in (
            block_of_slot,
            grad,
            left_basis.reshape(by_core),
            right_basis,
            left_gram,
            right_gram,
            moment_first,
            moment_second,
        )
    ]
    codes, scales, rows_of_first, nlgram, nrgram, nfirst, nsecond = pl.pallas_call(
        exchange_kernel,
        out_shape=(
            pltpu.VMEM((2, DEV, 8, 128), jnp.int32),
            pltpu.VMEM((DEV, 1, 128), F32),
            pltpu.VMEM((DEV, 16, 128), F32),
            pltpu.VMEM(square, F32),
            pltpu.VMEM(square, F32),
            pltpu.VMEM(square, F32),
            pltpu.VMEM(square, F32),
        ),
        in_specs=[hbm] * 8,
        out_specs=(vmem,) * 7,
        scratch_shapes=[pltpu.SMEM((blocks,), jnp.int32), pltpu.VMEM((blocks, 16, 128), BF16)]
        + [pltpu.VMEM(by_core, F32)]
        + [pltpu.VMEM(square, F32)] * 5
        + [pltpu.VMEM((2, 2, N, N // 2), BF16)] * 2
        + [pltpu.VMEM(by_core, BF16)] * 2
        + [pltpu.VMEM(square, BF16)] * 2
        + [
            pltpu.VMEM((2, DEV, 16, 128), BF16),
            pltpu.VMEM((2, DP // 2, 2, TP, 16, 128), BF16),
            pltpu.VMEM(by_core, BF16),
            pltpu.VMEM((N, N), BF16),
            pltpu.VMEM((N, N), BF16),
            pltpu.VMEM((2, DP // 2, 2, TP, 8, 128), jnp.int32),
            pltpu.VMEM((2, 4, 1, 128), F32),
            pltpu.VMEM((2, 1, N // 2), F32),
            pltpu.SemaphoreType.DMA((8,)),
            pltpu.SemaphoreType.DMA((2, 4)),
            pltpu.SemaphoreType.DMA((2, 2)),
            pltpu.SemaphoreType.DMA((2,)),
            pltpu.SemaphoreType.DMA((2,)),
            pltpu.SemaphoreType.DMA((2,)),
        ],
        compiler_params=pltpu.CompilerParams(collective_id=0, has_side_effects=True, vmem_limit_bytes=44 << 20),
        name="exchange",
    )(*operands)
    update, *rest = pl.pallas_call(
        finish_kernel,
        out_shape=(jax.ShapeDtypeStruct((blocks, 16, 128), F32),) + (jax.ShapeDtypeStruct(square, F32),) * 4,
        in_specs=[hbm] + [vmem] * 7,
        out_specs=(hbm,) * 5,
        scratch_shapes=[
            pltpu.SMEM((blocks,), jnp.int32),
            pltpu.VMEM((DEV, 16, 128), F32),
            pltpu.SemaphoreType.DMA((6,)),
        ],
        compiler_params=pltpu.CompilerParams(vmem_limit_bytes=16 << 20),
        name="finish",
    )(operands[0], codes, scales, rows_of_first, nlgram, nrgram, nfirst, nsecond)
    update = update.reshape(blocks, 4, 4, 128).transpose(0, 2, 1, 3).reshape(blocks, 4, N)
    return (update, *rest)


def solution(mesh):
    owner = P(("dp", "tensor"), None, None)
    rows = P(None, ("dp", "tensor"), None)
    return jax.shard_map(
        local,
        mesh=mesh,
        in_specs=(rows, P(), owner, owner, owner, owner, owner, owner),
        out_specs=(rows, owner, owner, owner, owner),
        check_vma=False,
    )
```

```python
import jax
import jax.numpy as jnp
from jax import lax
from jax.experimental import pallas as pl
from jax.experimental.pallas import tpu as pltpu
from jax.sharding import PartitionSpec as P

MESH = pl.DeviceIdType.MESH
F32 = jnp.float32
BF16 = jnp.bfloat16
N = 512
DP, TP = 16, 8
DEV = DP * TP
LEVELS = 32767.0


def split(x):
    hi = x.astype(BF16)
    return hi, (x - hi.astype(F32)).astype(BF16)


def dot(a, b):
    return jnp.dot(a, b, preferred_element_type=F32)


def dot_nt(a, b):
    return lax.dot_general(a, b, (((1,), (1,)), ((), ())), preferred_element_type=F32)


def dot_tn(a, b):
    return lax.dot_general(a, b, (((0,), (0,)), ((), ())), preferred_element_type=F32)


def scale_lanes(dp, tp, s):
    lane = lax.broadcasted_iota(jnp.int32, (8, 128), 1)
    row = lax.broadcasted_iota(jnp.int32, (8, 128), 0)
    return lane == 64 * s + (((dp // 2) & 1) * TP + tp) * 4 + (row & 3)


def decode(code, scale, mine):
    step = jnp.sum(jnp.where(mine, jnp.broadcast_to(scale, (8, 128)), 0.0), axis=1, keepdims=True)
    return ((code << 16) >> 16).astype(F32) * step, (code >> 16).astype(F32) * step


def exchange_kernel(
    bos_h,
    grad_h,
    left_h,
    right_h,
    lgram_h,
    rgram_h,
    first_h,
    second_h,
    codes,
    scales,
    rows_of_first,
    nlgram,
    nrgram,
    nfirst,
    nsecond,
    bos,
    grad,
    left,
    right,
    lgram,
    rgram,
    first,
    second,
    lt_hi,
    lt_lo,
    l_hi,
    l_lo,
    r_hi,
    r_lo,
    stage_in,
    land_in,
    owned,
    n_hi,
    n_lo,
    stage_out,
    stage_scale,
    step_of_first,
    load_sem,
    in_send,
    in_recv,
    out_send,
    out_recv,
    sc_sem,
):
    dp = lax.axis_index("dp")
    tp = lax.axis_index("tensor")
    me = dp * TP + tp

    loads = [
        pltpu.make_async_copy(src, dst, load_sem.at[i])
        for i, (src, dst) in enumerate(
            (
                (bos_h, bos),
                (grad_h, grad),
                (left_h, left),
                (right_h, right),
                (first_h, first),
                (second_h, second),
                (lgram_h, lgram),
                (rgram_h, rgram),
            )
        )
    ]
    for load in loads[:2]:
        load.start()

    barrier = pltpu.get_barrier_semaphore()

    def greet(d, t):
        pl.semaphore_signal(barrier, inc=1, device_id=(d, t), device_id_type=MESH)

    for i in range(1, TP):
        greet(dp, (tp + i) & (TP - 1))

    @pl.loop(1, DP)
    def _(j):
        for i in range(TP):
            greet((dp + j) & (DP - 1), (tp + i) & (TP - 1))

    for load in loads[2:]:
        load.start()

    loads[0].wait()
    loads[1].wait()
    def gather(s):
        @pl.loop(0, DEV, step=8)
        def _(p):
            for i in range(8):
                stage_in[s, p + i] = grad[bos[2 * (p + i) + s]]

        land_in[s, dp // 2, dp & 1, tp] = stage_in[s, me]

    gather(0)
    pl.semaphore_wait(barrier, DEV - 1)

    def send_in(s, part):
        def one(d, t):
            pltpu.make_async_remote_copy(
                stage_in.at[s, d * TP + t],
                land_in.at[s, dp // 2, dp & 1, tp],
                in_send.at[s, part],
                in_recv.at[s, part // 2],
                device_id=(d, t),
                device_id_type=MESH,
            ).start()

        if part == 0:
            for i in range(1, TP):
                one(dp, (tp + i) & (TP - 1))

        @pl.loop(1 if part == 0 else 0, 4)
        def _(k):
            j = 8 * (part % 2) + 2 * k + part // 2
            for i in range(TP):
                one((dp + j) & (DP - 1), (tp + i) & (TP - 1))

    def all_of(ref, sem):
        pltpu.make_async_copy(ref, ref, sem).wait()

    def sent_in(s, part):
        all_of(stage_in.at[s, pl.ds(0, DEV // 4 - (part == 0))], in_send.at[s, part])

    for part in range(4):
        send_in(0, part)
    gather(1)

    loads[2].wait()
    loads[3].wait()
    for s in range(2):

        @pl.loop(0, 4)
        def _(r):
            rows = pl.ds(pl.multiple_of(r * 128, 128), 128)
            hi, lo = split(right[s, rows, :])
            r_hi[s, rows, :] = hi
            r_lo[s, rows, :] = lo
            hi, lo = split(left[s, pl.ds(2 * r, 2)])
            l_hi[s, pl.ds(2 * r, 2)] = hi
            l_lo[s, pl.ds(2 * r, 2)] = lo
            for c in range(2):
                hi, lo = split(left[s, :, c, :, rows].reshape(N // 2, 128).T)
                lt_hi[s, c, rows, :] = hi
                lt_lo[s, c, rows, :] = lo

    loads[4].wait()
    loads[5].wait()

    for part in range(3):
        sent_in(0, part)
    send_in(1, 0)
    sent_in(0, 3)
    for part in range(1, 4):
        send_in(1, part)

    for s in range(2):
        half = []
        for j in range(2):
            c = (dp + j) & 1
            all_of(stage_in.at[s, pl.ds(0, DEV // 2 - 1 + j)], in_recv.at[s, j])
            for k in range(4):
                owned[s, :, c, :, k * 128 : (k + 1) * 128] = land_in[s, :, c, :, 4 * k : 4 * k + 4, :].reshape(
                    DP // 2, 4 * TP, 128
                )
            block = owned[s, :, c].reshape(N // 2, N)
            part_hi, part_lo = split(dot(block, r_hi[s]) + dot(block, r_lo[s]))
            half.append(
                dot(lt_hi[s, c], part_hi) + (dot(lt_hi[s, c], part_lo) + dot(lt_lo[s, c], part_hi))
            )
        rotated = half[0] + half[1]
        nf = 0.9 * first[s] + 0.1 * rotated
        ns = 0.95 * second[s] + 0.05 * rotated * rotated
        nfirst[s] = nf
        nsecond[s] = ns
        hi, lo = split(nf / (jnp.sqrt(ns) + 1e-08))
        n_hi[...] = hi
        n_lo[...] = lo

        for j in range(2):
            c = (dp + j) & 1
            left_hi = l_hi[s, :, c].reshape(N // 2, N)
            left_lo = l_lo[s, :, c].reshape(N // 2, N)
            hi, lo = split(dot(left_hi, n_hi[...]) + (dot(left_hi, n_lo[...]) + dot(left_lo, n_hi[...])))
            result = dot_nt(hi, r_hi[s]) + (dot_nt(hi, r_lo[s]) + dot_nt(lo, r_hi[s]))
            top = jnp.maximum(jnp.max(jnp.abs(result), axis=1, keepdims=True), 1e-33)
            q = jnp.clip(jnp.round(result * (LEVELS / top)), -LEVELS, LEVELS).astype(jnp.int32)
            packed = (q[:, : N // 2] & 0xFFFF) | (q[:, N // 2 :] << 16)
            for h in range(2):
                stage_out[s, :, c, :, 4 * h : 4 * h + 4, :] = packed[:, h * 128 : (h + 1) * 128].reshape(
                    DP // 2, TP, 4, 128
                )
            step = jnp.broadcast_to(top * (1.0 / LEVELS), (N // 2, 128)).T
            if s == 0:
                step_of_first[c] = step[:1, :]
            else:
                for h in range(4):
                    part = slice(64 * h, 64 * h + 64)
                    stage_scale[c, h] = jnp.concatenate([step_of_first[c][:, part], step[:1, part]], axis=1)

            def send_out(g, t):
                pltpu.make_async_remote_copy(
                    stage_out.at[s, g, c, t],
                    codes.at[s, me],
                    out_send.at[s],
                    out_recv.at[s],
                    device_id=(2 * g + c, t),
                    device_id_type=MESH,
                ).start()

            def send_scale(g, t):
                pltpu.make_async_remote_copy(
                    stage_scale.at[c, g // 2],
                    scales.at[me],
                    sc_sem.at[0],
                    sc_sem.at[1],
                    device_id=(2 * g + c, t),
                    device_id_type=MESH,
                ).start()

            def to_all(send):
                for i in range(1 if j == 0 else 0, TP):
                    send(dp // 2, (tp + i) & (TP - 1))

                @pl.loop(1, DP // 2)
                def _(a):
                    for i in range(TP):
                        send((dp // 2 + a) & (DP // 2 - 1), (tp + i) & (TP - 1))

            if s == 1 and j == 1:
                to_all(send_scale)
            to_all(send_out)
            if s == 1 and j == 0:
                to_all(send_scale)

        codes[s, me] = stage_out[s, dp // 2, dp & 1, tp]

    scales[me] = stage_scale[dp & 1, dp // 4]

    loads[6].wait()
    loads[7].wait()
    for s in range(2):
        block = owned[s].reshape(N, N)
        nlgram[s] = 0.95 * lgram[s] + 0.05 * dot_nt(block, block)
        nrgram[s] = 0.95 * rgram[s] + 0.05 * dot_tn(block, block)
    all_of(scales.at[pl.ds(0, DEV - 1)], sc_sem.at[1])
    all_of(codes.at[0, pl.ds(0, DEV - 1)], out_recv.at[0])
    mine = scale_lanes(dp, tp, 0)

    @pl.loop(0, DEV, step=16)
    def _(p):
        for i in range(16):
            low, high = decode(codes[0, p + i], scales[p + i], mine)
            rows_of_first[p + i, 0:8, :] = low
            rows_of_first[p + i, 8:16, :] = high

    for part in range(4):
        sent_in(1, part)
    all_of(scales.at[pl.ds(0, DEV - 1)], sc_sem.at[0])
    for s in range(2):
        all_of(codes.at[s, pl.ds(0, DEV - 1)], out_send.at[s])
    all_of(codes.at[1, pl.ds(0, DEV - 1)], out_recv.at[1])


def finish_kernel(
    bos_h, codes, scales, rows_of_first, nlgram, nrgram, nfirst, nsecond, update, o_l, o_r, o_f, o_s, bos, rows, sem
):
    dp = lax.axis_index("dp")
    tp = lax.axis_index("tensor")
    load = pltpu.make_async_copy(bos_h, bos, sem.at[5])
    load.start()
    moves = [
        pltpu.make_async_copy(src, dst, sem.at[i])
        for i, (src, dst) in enumerate(((nlgram, o_l), (nrgram, o_r), (nfirst, o_f), (nsecond, o_s)))
    ]
    for move in moves:
        move.start()
    mine = scale_lanes(dp, tp, 1)
    load.wait()

    @pl.loop(0, DEV, step=32)
    def _(p):
        for i in range(32):
            rows[bos[2 * (p + i)]] = rows_of_first[p + i]

    @pl.loop(0, DEV, step=32)
    def _(p):
        for i in range(32):
            low, high = decode(codes[1, p + i], scales[p + i], mine)
            b = bos[2 * (p + i) + 1]
            rows[b, 0:8, :] = low
            rows[b, 8:16, :] = high

    out = pltpu.make_async_copy(rows, update, sem.at[4])
    out.start()
    for move in moves:
        move.wait()
    out.wait()


def local(grad_blocks, block_of_slot, left_basis, right_basis, left_gram, right_gram, moment_first, moment_second):
    blocks = grad_blocks.shape[0]
    grad = grad_blocks.reshape(blocks, 4, 4, 128).transpose(0, 2, 1, 3).reshape(blocks, 16, 128)
    hbm = pl.BlockSpec(memory_space=pltpu.HBM)
    vmem = pl.BlockSpec(memory_space=pltpu.VMEM)
    square = (2, N, N)
    by_core = (2, DP // 2, 2, 4 * TP, N)
    operands = [
        pltpu.with_memory_space_constraint(x, pltpu.HBM)
        for x in (
            block_of_slot,
            grad,
            left_basis.reshape(by_core),
            right_basis,
            left_gram,
            right_gram,
            moment_first,
            moment_second,
        )
    ]
    codes, scales, rows_of_first, nlgram, nrgram, nfirst, nsecond = pl.pallas_call(
        exchange_kernel,
        out_shape=(
            pltpu.VMEM((2, DEV, 8, 128), jnp.int32),
            pltpu.VMEM((DEV, 1, 128), F32),
            pltpu.VMEM((DEV, 16, 128), F32),
            pltpu.VMEM(square, F32),
            pltpu.VMEM(square, F32),
            pltpu.VMEM(square, F32),
            pltpu.VMEM(square, F32),
        ),
        in_specs=[hbm] * 8,
        out_specs=(vmem,) * 7,
        scratch_shapes=[pltpu.SMEM((blocks,), jnp.int32), pltpu.VMEM((blocks, 16, 128), BF16)]
        + [pltpu.VMEM(by_core, F32)]
        + [pltpu.VMEM(square, F32)] * 5
        + [pltpu.VMEM((2, 2, N, N // 2), BF16)] * 2
        + [pltpu.VMEM(by_core, BF16)] * 2
        + [pltpu.VMEM(square, BF16)] * 2
        + [
            pltpu.VMEM((2, DEV, 16, 128), BF16),
            pltpu.VMEM((2, DP // 2, 2, TP, 16, 128), BF16),
            pltpu.VMEM(by_core, BF16),
            pltpu.VMEM((N, N), BF16),
            pltpu.VMEM((N, N), BF16),
            pltpu.VMEM((2, DP // 2, 2, TP, 8, 128), jnp.int32),
            pltpu.VMEM((2, 4, 1, 128), F32),
            pltpu.VMEM((2, 1, N // 2), F32),
            pltpu.SemaphoreType.DMA((8,)),
            pltpu.SemaphoreType.DMA((2, 4)),
            pltpu.SemaphoreType.DMA((2, 2)),
            pltpu.SemaphoreType.DMA((2,)),
            pltpu.SemaphoreType.DMA((2,)),
            pltpu.SemaphoreType.DMA((2,)),
        ],
        compiler_params=pltpu.CompilerParams(collective_id=0, has_side_effects=True, vmem_limit_bytes=44 << 20),
        name="exchange",
    )(*operands)
    update, *rest = pl.pallas_call(
        finish_kernel,
        out_shape=(jax.ShapeDtypeStruct((blocks, 16, 128), F32),) + (jax.ShapeDtypeStruct(square, F32),) * 4,
        in_specs=[hbm] + [vmem] * 7,
        out_specs=(hbm,) * 5,
        scratch_shapes=[
            pltpu.SMEM((blocks,), jnp.int32),
            pltpu.VMEM((blocks, 16, 128), F32),
            pltpu.SemaphoreType.DMA((6,)),
        ],
        compiler_params=pltpu.CompilerParams(vmem_limit_bytes=16 << 20),
        name="finish",
    )(operands[0], codes, scales, rows_of_first, nlgram, nrgram, nfirst, nsecond)
    update = update.reshape(blocks, 4, 4, 128).transpose(0, 2, 1, 3).reshape(blocks, 4, N)
    return (update, *rest)


def solution(mesh):
    owner = P(("dp", "tensor"), None, None)
    rows = P(None, ("dp", "tensor"), None)
    return jax.shard_map(
        local,
        mesh=mesh,
        in_specs=(rows, P(), owner, owner, owner, owner, owner, owner),
        out_specs=(rows, owner, owner, owner, owner),
        check_vma=False,
    )
```

```python
import jax
import jax.numpy as jnp
from jax import lax
from jax.experimental import pallas as pl
from jax.experimental.pallas import tpu as pltpu
from jax.sharding import PartitionSpec as P

MESH = pl.DeviceIdType.MESH
F32 = jnp.float32
BF16 = jnp.bfloat16
N = 512
DP, TP = 16, 8
DEV = DP * TP
LEVELS = 32767.0


def split(x):
    hi = x.astype(BF16)
    return hi, (x - hi.astype(F32)).astype(BF16)


def dot(a, b):
    return jnp.dot(a, b, preferred_element_type=F32)


def dot_nt(a, b):
    return lax.dot_general(a, b, (((1,), (1,)), ((), ())), preferred_element_type=F32)


def dot_tn(a, b):
    return lax.dot_general(a, b, (((0,), (0,)), ((), ())), preferred_element_type=F32)


def scale_lanes(dp, tp, s):
    lane = lax.broadcasted_iota(jnp.int32, (8, 128), 1)
    row = lax.broadcasted_iota(jnp.int32, (8, 128), 0)
    return lane == 64 * s + (((dp // 2) & 1) * TP + tp) * 4 + (row & 3)


def decode(code, scale, mine):
    step = jnp.sum(jnp.where(mine, jnp.broadcast_to(scale, (8, 128)), 0.0), axis=1, keepdims=True)
    return ((code << 16) >> 16).astype(F32) * step, (code >> 16).astype(F32) * step


def exchange_kernel(
    bos_h,
    grad_h,
    left_h,
    right_h,
    lgram_h,
    rgram_h,
    first_h,
    second_h,
    codes,
    scales,
    rows_of_first,
    nlgram,
    nrgram,
    nfirst,
    nsecond,
    bos,
    grad,
    left,
    right,
    lgram,
    rgram,
    first,
    second,
    lt_hi,
    lt_lo,
    l_hi,
    l_lo,
    r_hi,
    r_lo,
    stage_in,
    land_in,
    owned,
    n_hi,
    n_lo,
    stage_out,
    stage_scale,
    step_of_first,
    load_sem,
    in_send,
    in_recv,
    out_send,
    out_recv,
    sc_sem,
):
    dp = lax.axis_index("dp")
    tp = lax.axis_index("tensor")
    me = dp * TP + tp

    loads = [
        pltpu.make_async_copy(src, dst, load_sem.at[i])
        for i, (src, dst) in enumerate(
            (
                (bos_h, bos),
                (grad_h, grad),
                (left_h, left),
                (right_h, right),
                (first_h, first),
                (second_h, second),
                (lgram_h, lgram),
                (rgram_h, rgram),
            )
        )
    ]
    for load in loads[:2]:
        load.start()

    barrier = pltpu.get_barrier_semaphore()

    def greet(d, t):
        pl.semaphore_signal(barrier, inc=1, device_id=(d, t), device_id_type=MESH)

    for i in range(1, TP):
        greet(dp, (tp + i) & (TP - 1))

    @pl.loop(1, DP)
    def _(j):
        for i in range(TP):
            greet((dp + j) & (DP - 1), (tp + i) & (TP - 1))

    for load in loads[2:]:
        load.start()

    loads[0].wait()
    loads[1].wait()
    def gather(s):
        @pl.loop(0, DEV, step=8)
        def _(p):
            for i in range(8):
                stage_in[s, p + i] = grad[bos[2 * (p + i) + s]]

        land_in[s, dp // 2, dp & 1, tp] = stage_in[s, me]

    gather(0)
    pl.semaphore_wait(barrier, DEV - 1)

    def send_in(s, part):
        def one(d, t):
            pltpu.make_async_remote_copy(
                stage_in.at[s, d * TP + t],
                land_in.at[s, dp // 2, dp & 1, tp],
                in_send.at[s, part],
                in_recv.at[s, part // 2],
                device_id=(d, t),
                device_id_type=MESH,
            ).start()

        if part == 0:
            for i in range(1, TP):
                one(dp, (tp + i) & (TP - 1))

        @pl.loop(1 if part == 0 else 0, 4)
        def _(k):
            j = 8 * (part % 2) + 2 * k + part // 2
            for i in range(TP):
                one((dp + j) & (DP - 1), (tp + i) & (TP - 1))

    def all_of(ref, sem):
        pltpu.make_async_copy(ref, ref, sem).wait()

    def sent_in(s, part):
        all_of(stage_in.at[s, pl.ds(0, DEV // 4 - (part == 0))], in_send.at[s, part])

    for part in range(4):
        send_in(0, part)
    gather(1)

    loads[2].wait()
    loads[3].wait()
    for s in range(2):

        @pl.loop(0, 4)
        def _(r):
            rows = pl.ds(pl.multiple_of(r * 128, 128), 128)
            hi, lo = split(right[s, rows, :])
            r_hi[s, rows, :] = hi
            r_lo[s, rows, :] = lo
            hi, lo = split(left[s, pl.ds(2 * r, 2)])
            l_hi[s, pl.ds(2 * r, 2)] = hi
            l_lo[s, pl.ds(2 * r, 2)] = lo
            for c in range(2):
                hi, lo = split(left[s, :, c, :, rows].reshape(N // 2, 128).T)
                lt_hi[s, c, rows, :] = hi
                lt_lo[s, c, rows, :] = lo

    loads[4].wait()
    loads[5].wait()
    for part in range(3):
        sent_in(0, part)
    send_in(1, 0)
    sent_in(0, 3)
    for part in range(1, 4):
        send_in(1, part)

    for s in range(2):

        @pl.loop(0, 4)
        def _(r):
            rows = pl.ds(pl.multiple_of(r * 128, 128), 128)
            first[s, rows, :] = 0.9 * first[s, rows, :]
            second[s, rows, :] = 0.95 * second[s, rows, :]

    for s in range(2):
        half = []
        for j in range(2):
            c = (dp + j) & 1
            all_of(stage_in.at[s, pl.ds(0, DEV // 2 - 1 + j)], in_recv.at[s, j])
            for k in range(4):
                owned[s, :, c, :, k * 128 : (k + 1) * 128] = land_in[s, :, c, :, 4 * k : 4 * k + 4, :].reshape(
                    DP // 2, 4 * TP, 128
                )
            block = owned[s, :, c].reshape(N // 2, N)
            part_hi, part_lo = split(dot(block, r_hi[s]) + dot(block, r_lo[s]))
            half.append(
                dot(lt_hi[s, c], part_hi) + (dot(lt_hi[s, c], part_lo) + dot(lt_lo[s, c], part_hi))
            )
        rotated = half[0] + half[1]
        nf = first[s] + 0.1 * rotated
        ns = second[s] + 0.05 * rotated * rotated
        nfirst[s] = nf
        nsecond[s] = ns
        hi, lo = split(nf / (jnp.sqrt(ns) + 1e-08))
        n_hi[...] = hi
        n_lo[...] = lo

        for j in range(2):
            c = (dp + j) & 1
            left_hi = l_hi[s, :, c].reshape(N // 2, N)
            left_lo = l_lo[s, :, c].reshape(N // 2, N)
            hi, lo = split(dot(left_hi, n_hi[...]) + (dot(left_hi, n_lo[...]) + dot(left_lo, n_hi[...])))
            result = dot_nt(hi, r_hi[s]) + (dot_nt(hi, r_lo[s]) + dot_nt(lo, r_hi[s]))
            top = jnp.maximum(jnp.max(jnp.abs(result), axis=1, keepdims=True), 1e-33)
            q = jnp.clip(jnp.round(result * (LEVELS / top)), -LEVELS, LEVELS).astype(jnp.int32)
            packed = (q[:, : N // 2] & 0xFFFF) | (q[:, N // 2 :] << 16)
            for h in range(2):
                stage_out[s, :, c, :, 4 * h : 4 * h + 4, :] = packed[:, h * 128 : (h + 1) * 128].reshape(
                    DP // 2, TP, 4, 128
                )
            step = jnp.broadcast_to(top * (1.0 / LEVELS), (N // 2, 128)).T
            if s == 0:
                step_of_first[c] = step[:1, :]
            else:
                for h in range(4):
                    part = slice(64 * h, 64 * h + 64)
                    stage_scale[c, h] = jnp.concatenate([step_of_first[c][:, part], step[:1, part]], axis=1)

            def send_out(g, t):
                pltpu.make_async_remote_copy(
                    stage_out.at[s, g, c, t],
                    codes.at[s, me],
                    out_send.at[s],
                    out_recv.at[s],
                    device_id=(2 * g + c, t),
                    device_id_type=MESH,
                ).start()

            def send_scale(g, t):
                pltpu.make_async_remote_copy(
                    stage_scale.at[c, g // 2],
                    scales.at[me],
                    sc_sem.at[0],
                    sc_sem.at[1],
                    device_id=(2 * g + c, t),
                    device_id_type=MESH,
                ).start()

            def to_all(send):
                for i in range(1 if j == 0 else 0, TP):
                    send(dp // 2, (tp + i) & (TP - 1))

                @pl.loop(1, DP // 2)
                def _(a):
                    for i in range(TP):
                        send((dp // 2 + a) & (DP // 2 - 1), (tp + i) & (TP - 1))

            if s == 1 and j == 1:
                to_all(send_scale)
            to_all(send_out)
            if s == 1 and j == 0:
                to_all(send_scale)

        codes[s, me] = stage_out[s, dp // 2, dp & 1, tp]

    scales[me] = stage_scale[dp & 1, dp // 4]

    loads[6].wait()
    loads[7].wait()
    for s in range(2):
        block = owned[s].reshape(N, N)
        nlgram[s] = 0.95 * lgram[s] + 0.05 * dot_nt(block, block)
        nrgram[s] = 0.95 * rgram[s] + 0.05 * dot_tn(block, block)
    all_of(scales.at[pl.ds(0, DEV - 1)], sc_sem.at[1])
    all_of(codes.at[0, pl.ds(0, DEV - 1)], out_recv.at[0])
    mine = scale_lanes(dp, tp, 0)

    @pl.loop(0, DEV, step=16)
    def _(p):
        for i in range(16):
            low, high = decode(codes[0, p + i], scales[p + i], mine)
            rows_of_first[p + i, 0:8, :] = low
            rows_of_first[p + i, 8:16, :] = high

    for part in range(4):
        sent_in(1, part)
    all_of(scales.at[pl.ds(0, DEV - 1)], sc_sem.at[0])
    for s in range(2):
        all_of(codes.at[s, pl.ds(0, DEV - 1)], out_send.at[s])
    all_of(codes.at[1, pl.ds(0, DEV - 1)], out_recv.at[1])


def finish_kernel(
    bos_h, codes, scales, rows_of_first, nlgram, nrgram, nfirst, nsecond, update, o_l, o_r, o_f, o_s, bos, rows, sem
):
    dp = lax.axis_index("dp")
    tp = lax.axis_index("tensor")
    load = pltpu.make_async_copy(bos_h, bos, sem.at[5])
    load.start()
    moves = [
        pltpu.make_async_copy(src, dst, sem.at[i])
        for i, (src, dst) in enumerate(((nlgram, o_l), (nrgram, o_r), (nfirst, o_f), (nsecond, o_s)))
    ]
    for move in moves:
        move.start()
    mine = scale_lanes(dp, tp, 1)
    load.wait()

    @pl.loop(0, DEV, step=32)
    def _(p):
        for i in range(32):
            rows[bos[2 * (p + i)]] = rows_of_first[p + i]

    @pl.loop(0, DEV, step=32)
    def _(p):
        for i in range(32):
            low, high = decode(codes[1, p + i], scales[p + i], mine)
            b = bos[2 * (p + i) + 1]
            rows[b, 0:8, :] = low
            rows[b, 8:16, :] = high

    out = pltpu.make_async_copy(rows, update, sem.at[4])
    out.start()
    for move in moves:
        move.wait()
    out.wait()


def local(grad_blocks, block_of_slot, left_basis, right_basis, left_gram, right_gram, moment_first, moment_second):
    blocks = grad_blocks.shape[0]
    grad = grad_blocks.reshape(blocks, 4, 4, 128).transpose(0, 2, 1, 3).reshape(blocks, 16, 128)
    hbm = pl.BlockSpec(memory_space=pltpu.HBM)
    vmem = pl.BlockSpec(memory_space=pltpu.VMEM)
    square = (2, N, N)
    by_core = (2, DP // 2, 2, 4 * TP, N)
    operands = [
        pltpu.with_memory_space_constraint(x, pltpu.HBM)
        for x in (
            block_of_slot,
            grad,
            left_basis.reshape(by_core),
            right_basis,
            left_gram,
            right_gram,
            moment_first,
            moment_second,
        )
    ]
    codes, scales, rows_of_first, nlgram, nrgram, nfirst, nsecond = pl.pallas_call(
        exchange_kernel,
        out_shape=(
            pltpu.VMEM((2, DEV, 8, 128), jnp.int32),
            pltpu.VMEM((DEV, 1, 128), F32),
            pltpu.VMEM((DEV, 16, 128), F32),
            pltpu.VMEM(square, F32),
            pltpu.VMEM(square, F32),
            pltpu.VMEM(square, F32),
            pltpu.VMEM(square, F32),
        ),
        in_specs=[hbm] * 8,
        out_specs=(vmem,) * 7,
        scratch_shapes=[pltpu.SMEM((blocks,), jnp.int32), pltpu.VMEM((blocks, 16, 128), BF16)]
        + [pltpu.VMEM(by_core, F32)]
        + [pltpu.VMEM(square, F32)] * 5
        + [pltpu.VMEM((2, 2, N, N // 2), BF16)] * 2
        + [pltpu.VMEM(by_core, BF16)] * 2
        + [pltpu.VMEM(square, BF16)] * 2
        + [
            pltpu.VMEM((2, DEV, 16, 128), BF16),
            pltpu.VMEM((2, DP // 2, 2, TP, 16, 128), BF16),
            pltpu.VMEM(by_core, BF16),
            pltpu.VMEM((N, N), BF16),
            pltpu.VMEM((N, N), BF16),
            pltpu.VMEM((2, DP // 2, 2, TP, 8, 128), jnp.int32),
            pltpu.VMEM((2, 4, 1, 128), F32),
            pltpu.VMEM((2, 1, N // 2), F32),
            pltpu.SemaphoreType.DMA((8,)),
            pltpu.SemaphoreType.DMA((2, 4)),
            pltpu.SemaphoreType.DMA((2, 2)),
            pltpu.SemaphoreType.DMA((2,)),
            pltpu.SemaphoreType.DMA((2,)),
            pltpu.SemaphoreType.DMA((2,)),
        ],
        compiler_params=pltpu.CompilerParams(collective_id=0, has_side_effects=True, vmem_limit_bytes=44 << 20),
        name="exchange",
    )(*operands)
    update, *rest = pl.pallas_call(
        finish_kernel,
        out_shape=(jax.ShapeDtypeStruct((blocks, 16, 128), F32),) + (jax.ShapeDtypeStruct(square, F32),) * 4,
        in_specs=[hbm] + [vmem] * 7,
        out_specs=(hbm,) * 5,
        scratch_shapes=[
            pltpu.SMEM((blocks,), jnp.int32),
            pltpu.VMEM((blocks, 16, 128), F32),
            pltpu.SemaphoreType.DMA((6,)),
        ],
        compiler_params=pltpu.CompilerParams(vmem_limit_bytes=16 << 20),
        name="finish",
    )(operands[0], codes, scales, rows_of_first, nlgram, nrgram, nfirst, nsecond)
    update = update.reshape(blocks, 4, 4, 128).transpose(0, 2, 1, 3).reshape(blocks, 4, N)
    return (update, *rest)


def solution(mesh):
    owner = P(("dp", "tensor"), None, None)
    rows = P(None, ("dp", "tensor"), None)
    return jax.shard_map(
        local,
        mesh=mesh,
        in_specs=(rows, P(), owner, owner, owner, owner, owner, owner),
        out_specs=(rows, owner, owner, owner, owner),
        check_vma=False,
    )
```
